32 devices in a mesh: row: 4 (over x, core), col: 8 (over z, y).
Axes of the slice: x: 2, y: 2, z: 4, core: 2. Of those that a mesh axis runs over, the one named last changes fastest.
Arguments:
- raw_vectors: float32 [2048, 81920], P('col', 'row'), may hold values from -810 to 810
- interval_count: int32 [8], replicated, may hold values from 1 to 256, 1024 in all
- cluster_of: int32 [8, 256], P('col'), may hold values from 0 to 31, never falling along the last dimension, each value on 1 to 32 neighbouring positions
- panel_one: float32 [81920, 256], P(('row', 'col')), may hold values from -0.03125 to 0.03125
- factor_one: float32 [256, 256], replicated, may hold values from -0.3 to 2
- panel_two: float32 [81920, 256], P(('row', 'col')), may hold values from -0.03125 to 0.03125
- factor_two: float32 [256, 256], replicated, may hold values from -0.3 to 2
Outputs:
- eigenvectors: float32 [1024, 81920], P('col', 'row')
The draws below stay inside these ranges and needn't reach their ends.
Inputs may be any that keep to these rules, and one draw needn't show every extreme that they name: `interval_count`: the counts sum to 1024; one is exactly 256. `cluster_of`: labels never fall along an interval's slots; one label covers at most 32 slots, and one covers exactly 32.
All inputs are finite; a program needn't handle non-finite values.
Results may differ from the reference program's by a relative error of at most 0.0003.
Values sent between devices are 32-bit elements; how exact they have to be, the bound alone decides.
No kernel may reach another device: no remote copies, remote signals or barrier semaphores. Data moves between devices by JAX's collectives and lax.ppermute only.
A program may use at most 128 MiB of HBM per device.

```python
import math
import jax
import jax.numpy as jnp
import numpy as np
from jax import lax

N = 81920
R = 256
NB = 16
KD = 128
CAP = 256
K = 1024
SLOTS = 2048
CLUSTERS = 32
CMAX = 32
N_COL = 8


def draw_raw_vectors(key, part):
    key = jax.random.fold_in(key, 13)
    base_key, scale_key, row_key = jax.random.split(key, 3)
    base = jnp.clip(jax.random.normal(base_key, (SLOTS + 1, N), jnp.float32), -6.0, 6.0)
    slot_scale = jnp.exp(jax.random.uniform(scale_key, (SLOTS, 1), jnp.float32, 0.0, math.log(10.0)))
    rising = 1.0 + 2.0 * jnp.arange(N, dtype=jnp.float32)[None, :] / N
    row_scale = jnp.exp(jax.random.uniform(row_key, (1, N), jnp.float32, 0.0, math.log(3.0))) * rising
    return slot_scale * row_scale * (base[:-1] + 0.5 * base[1:])


def draw_factor_one(key, part):
    key = jax.random.fold_in(key, 21)
    diag_key, upper_key = jax.random.split(key, 2)
    diag_values = jax.random.uniform(diag_key, (R,), jnp.float32, 1.0, 2.0)
    upper_values = jnp.clip(0.05 * jax.random.normal(upper_key, (R, R), jnp.float32), -0.3, 0.3)
    upper = jnp.arange(R)[:, None] < jnp.arange(R)[None, :]
    return jnp.where(upper, upper_values, 0.0) + jnp.diag(diag_values)


def draw_factor_two(key, part):
    key = jax.random.fold_in(key, 22)
    diag_key, upper_key = jax.random.split(key, 2)
    diag_values = jax.random.uniform(diag_key, (R,), jnp.float32, 1.0, 2.0)
    upper_values = jnp.clip(0.05 * jax.random.normal(upper_key, (R, R), jnp.float32), -0.3, 0.3)
    upper = jnp.arange(R)[:, None] < jnp.arange(R)[None, :]
    return jnp.where(upper, upper_values, 0.0) + jnp.diag(diag_values)


def block_levels(stream_key, extent, cuts, least, top_value):
    level, own = 1.0, jax.random.fold_in(stream_key, 6)
    for position, shards_of in cuts:
        steps = jnp.exp(jax.random.uniform(jax.random.fold_in(own, position), (shards_of,), jnp.float32, least / len(cuts), top_value / len(cuts)))
        level = level * jnp.repeat(steps, extent[position] // shards_of).reshape([-1 if axis == position else 1 for axis in range(len(extent))])
    return level


def profile(number_of, total, reach, lean):
    weights = [(1 << 20) // math.isqrt(rank ** lean) + 1 for rank in range(2, number_of + 1)]
    surplus, given = total - reach - (number_of - 1), [1] * (number_of - 1)
    while surplus > 0:
        free = [i for i in range(number_of - 1) if given[i] < reach]
        mass, remaining = sum([weights[i] for i in free]), surplus
        for i in free:
            extra = min(reach - given[i], max(1, remaining * weights[i] // mass), surplus)
            given[i] = given[i] + extra
            surplus = surplus - extra
    return np.array([reach] + given)


def ragged(rng, number_of, total, most, slope):
    if number_of == 2:
        one = jax.random.randint(rng, (), max(1, total - most), min(most, total - 1) + 1)
        return jnp.stack([one, total - one])
    tallies = jnp.asarray(profile(number_of, total, most, slope), jnp.int32)
    couples = (number_of - 1) // 2
    source_of, receiver = tallies[1:1 + 2 * couples:2], tallies[2:2 + 2 * couples:2]
    slack = jnp.minimum(source_of - 1, most - receiver)
    moved = jax.random.randint(jax.random.fold_in(rng, 1), (couples,), 0, 1 << 20) % (slack + 1)
    tallies = tallies.at[1:1 + 2 * couples:2].set(source_of - moved).at[2:2 + 2 * couples:2].set(receiver + moved)
    return tallies[jax.random.permutation(jax.random.fold_in(rng, 2), number_of)]


def centred(rng, dims, scale, limit, shards=(), kind=jnp.bfloat16):
    result = scale * jax.random.normal(rng, dims, jnp.float32)
    if shards:
        result = result * block_levels(rng, dims, shards, -0.22, 0.18)
    return jnp.clip(result, -limit, limit).astype(kind)


def setup_inputs(seed: int = 0) -> dict:
    arg_keys = jax.random.split(jax.random.key(seed), 8)
    return {
        "raw_vectors": draw_raw_vectors(jax.random.fold_in(arg_keys[7], 71), 0),
        "interval_count": ragged(arg_keys[1], N_COL, K, CAP, 2).astype(jnp.int32),
        "cluster_of": jax.vmap(lambda own: jnp.searchsorted(jnp.cumsum(ragged(own, CLUSTERS, CAP, CMAX, 2)), jnp.arange(CAP), side="right"))(jax.random.split(arg_keys[2], N_COL)).reshape((N_COL, CAP)).astype(jnp.int32),
        "panel_one": centred(arg_keys[3], (N, R), (N // 2) ** -0.5, 0.03125, ((0, 32),), jnp.float32),
        "factor_one": draw_factor_one(jax.random.fold_in(arg_keys[7], 71), 0),
        "panel_two": centred(arg_keys[5], (N, R), (N // 2) ** -0.5, 0.03125, ((0, 32),), jnp.float32),
        "factor_two": draw_factor_two(jax.random.fold_in(arg_keys[7], 71), 0),
    }


highest = lax.Precision.HIGHEST

def block_order(counts, column_count, per_device, capacity):
    positions = jnp.arange(column_count * per_device, dtype=jnp.int32)
    device_of = positions // per_device
    local_index = positions % per_device
    rank_of = (local_index // NB * column_count + device_of) * NB + local_index % NB
    interval_end = jnp.cumsum(counts).astype(jnp.int32)
    interval_start = interval_end - counts
    owner_device = lax.optimization_barrier(jnp.sum((interval_end[None, :] <= rank_of[:, None]).astype(jnp.int32), axis=1))
    owner_hit = jnp.arange(column_count, dtype=jnp.int32)[None, :] == owner_device[:, None]
    owner_start = lax.optimization_barrier(jnp.sum(jnp.where(owner_hit, interval_start[None, :], 0), axis=1)).astype(jnp.int32)
    return (owner_device * capacity + rank_of - owner_start).astype(jnp.int32)

def finish_block(gram_full, raw_block, labels, is_alive):
    same_group = (labels[:, None] == labels[None, :]) & is_alive[:, None] & is_alive[None, :]
    alive_float = is_alive.astype(jnp.float32)
    masked = jnp.where(same_group, gram_full, 0.0) + jnp.diag(1.0 - alive_float)
    lower_factor = jnp.linalg.cholesky(masked)
    solved = jax.scipy.linalg.solve_triangular(lower_factor, raw_block, lower=True)
    return solved * math.sqrt(N)

def apply_panel(vectors, projected, reflectors, factor):
    scaled = jnp.dot(projected.astype(jnp.float32), factor.T.astype(jnp.float32), precision=highest, preferred_element_type=jnp.float32)
    return vectors - jnp.einsum('kr,nr->kn', scaled, reflectors, precision=highest)

def reference(raw_vectors, interval_count, cluster_of, panel_one, factor_one, panel_two, factor_two):
    blocks = raw_vectors.reshape(N_COL, CAP, N)
    alive_table = jnp.arange(CAP, dtype=jnp.int32)[None, :] < interval_count[:, None]

    def per_interval(members):
        raw_block, labels, is_alive = members
        gram_full = jnp.dot(raw_block.astype(jnp.float32), raw_block.T.astype(jnp.float32), precision=highest, preferred_element_type=jnp.float32)
        return finish_block(gram_full, raw_block, labels, is_alive)
    orthogonal = lax.map(per_interval, (blocks, cluster_of, alive_table)).reshape(SLOTS, N)
    wanted = block_order(interval_count, N_COL, KD, CAP)
    ordered = jnp.take(orthogonal, wanted, axis=0)
    for reflectors, factor in ((panel_two, factor_two), (panel_one, factor_one)):
        projected = jnp.dot(ordered.astype(jnp.float32), reflectors.astype(jnp.float32), precision=highest, preferred_element_type=jnp.float32)
        ordered = apply_panel(ordered, projected, reflectors, factor)
    return ordered
```

```python
import functools
import math

import jax
import jax.numpy as jnp
from jax import lax
from jax.experimental import pallas as pl
from jax.experimental.pallas import tpu as pltpu
from jax.sharding import PartitionSpec as P

N = 81920
NB = 16
KD = 128

highest = lax.Precision.HIGHEST


def dot_highest(a, b):
    return jnp.dot(a, b, precision=highest, preferred_element_type=jnp.float32)


def split_bf16(x):
    high = lax.reduce_precision(x, exponent_bits=8, mantissa_bits=7)
    return high.astype(jnp.bfloat16), (x - high).astype(jnp.bfloat16)


def swap(x, axis, step):
    size = lax.axis_size(axis)
    return lax.ppermute(x, axis, [(i, i ^ step) for i in range(size)])


def scatter_sum(x, axis, steps, index, unit):
    rows = x.shape[0] // (len(steps) + 1)
    total = lax.dynamic_slice_in_dim(x, index * rows, rows, 0)
    for step in steps:
        part = lax.dynamic_slice_in_dim(x, (index ^ step) * rows, rows, 0)
        total = total + swap(part, axis, step * unit)
    return total


def gather_rows(x, axis, steps, index, unit):
    rows = x.shape[0]
    whole = jnp.zeros(((len(steps) + 1) * rows,) + x.shape[1:], x.dtype)
    whole = lax.dynamic_update_slice_in_dim(whole, x, index * rows, 0)
    for step in steps:
        whole = lax.dynamic_update_slice_in_dim(whole, swap(x, axis, step * unit), (index ^ step) * rows, 0)
    return whole


def sum_everywhere(x):
    row_index, col_index = lax.axis_index("row"), lax.axis_index("col")
    stages = (
        ("row", range(1, 2), row_index % 2, 1),
        ("row", range(1, lax.axis_size("row") // 2), row_index // 2, 2),
        ("col", range(1, lax.axis_size("col")), col_index, 1),
    )
    for axis, steps, index, unit in stages:
        x = scatter_sum(x, axis, steps, index, unit)
    for axis, steps, index, unit in reversed(stages):
        x = gather_rows(x, axis, steps, index, unit)
    return x


def inverse_factor(gram_full, labels, is_alive):
    same_group = (labels[:, None] == labels[None, :]) & is_alive[:, None] & is_alive[None, :]
    alive_float = is_alive.astype(jnp.float32)
    masked = jnp.where(same_group, gram_full, 0.0) + jnp.diag(1.0 - alive_float)
    lower_factor = jnp.linalg.cholesky(masked)
    scaled_eye = math.sqrt(N) * jnp.eye(masked.shape[0], dtype=jnp.float32)
    return jax.scipy.linalg.solve_triangular(lower_factor, scaled_eye, lower=True)


def orthogonal_kernel(count, active_ref, owner_ref, factor_ref, high_ref, low_ref, *refs):
    blocks, ordered_ref, projected_ref, total = refs[:count], refs[count], refs[count + 1], refs[count + 2]
    window = NB * count

    @pl.when(pl.program_id(0) == 0)
    def _():
        projected_ref[...] = jnp.zeros_like(projected_ref)

    def one_window(j, carry):
        ranks = pl.ds(pl.multiple_of(j * window, window), window)
        local = pl.ds(pl.multiple_of(j * NB, NB), NB)
        total[...] = jnp.zeros_like(total)
        for k in range(count):

            @pl.when(active_ref[k, j] > 0)
            def _():
                factor = jnp.where(owner_ref[ranks, :] == k, factor_ref[ranks, :], 0.0)
                total[...] += dot_highest(factor, blocks[k][...])

        value = total[...]
        ordered_ref[:, local, :] = value.reshape(count, NB, value.shape[1])
        high = value.astype(jnp.bfloat16)
        low = (value - high.astype(jnp.float32)).astype(jnp.bfloat16)
        part = jnp.dot(high, high_ref[...], preferred_element_type=jnp.float32)
        part += jnp.dot(low, high_ref[...], preferred_element_type=jnp.float32)
        part += jnp.dot(high, low_ref[...], preferred_element_type=jnp.float32)
        projected_ref[:, local, :] += part.reshape(count, NB, part.shape[1])
        return carry

    lax.fori_loop(0, KD // NB, one_window, 0)


def orthogonalize(active, owner, factors, high, low, blocks):
    count, (capacity, width) = len(blocks), blocks[0].shape
    rank_total, reflectors = factors.shape[0], high.shape[1]
    tile = max(t for t in (128, 256, 512) if width % t == 0)
    whole = lambda shape: pl.BlockSpec(shape, lambda n, active: (0,) * len(shape))
    return pl.pallas_call(
        functools.partial(orthogonal_kernel, count),
        grid_spec=pltpu.PrefetchScalarGridSpec(
            num_scalar_prefetch=1,
            grid=(width // tile,),
            in_specs=[whole((rank_total, 1)), whole((rank_total, capacity))]
            + [pl.BlockSpec((tile, reflectors), lambda n, active: (n, 0))] * 2
            + [pl.BlockSpec((capacity, tile), lambda n, active: (0, n))] * count,
            out_specs=[
                pl.BlockSpec((count, KD, tile), lambda n, active: (0, 0, n)),
                whole((count, KD, reflectors)),
            ],
            scratch_shapes=[pltpu.VMEM((NB * count, tile), jnp.float32)],
        ),
        out_shape=[
            jax.ShapeDtypeStruct((count, KD, width), jnp.float32),
            jax.ShapeDtypeStruct((count, KD, reflectors), jnp.float32),
        ],
        compiler_params=pltpu.CompilerParams(vmem_limit_bytes=48 * 2**20),
    )(active, owner, factors, high, low, *blocks)


def body(raw_vectors, interval_count, cluster_of, panel_one, factor_one, panel_two, factor_two):
    column_count = lax.axis_size("col")
    column_index = lax.axis_index("col")
    capacity = raw_vectors.shape[0]
    width = panel_one.shape[0]
    columns = jnp.arange(column_count, dtype=jnp.int32)

    def column_block(k):
        return lax.dynamic_slice_in_dim(raw_vectors, (column_index ^ k) * width, width, 1)

    blocks = [column_block(0)] + [swap(column_block(k), "col", k) for k in range(1, column_count)]

    own_count = jnp.sum(jnp.where(columns == column_index, interval_count, 0))
    is_alive = jnp.arange(capacity, dtype=jnp.int32) < own_count
    gram_full = lax.psum(dot_highest(raw_vectors, raw_vectors.T), "row")
    inverse = inverse_factor(gram_full, cluster_of[0], is_alive)
    inverses = lax.all_gather(inverse, "col", axis=0, tiled=True)

    ranks = jnp.arange(column_count * KD, dtype=jnp.int32)
    interval_end = jnp.cumsum(interval_count).astype(jnp.int32)
    interval_start = interval_end - interval_count
    owner = jnp.sum((interval_end[None, :] <= ranks[:, None]).astype(jnp.int32), axis=1)
    owner_start = jnp.sum(jnp.where(columns[None, :] == owner[:, None], interval_start[None, :], 0), axis=1)
    factors = jnp.take(inverses, owner * capacity + ranks - owner_start, axis=0)
    window = NB * column_count
    window_start = jnp.arange(KD // NB, dtype=jnp.int32) * window
    overlap = (interval_start[:, None] < window_start[None, :] + window) & (
        interval_end[:, None] > window_start[None, :]
    )
    active = jnp.take(overlap.astype(jnp.int32), columns ^ column_index, axis=0)

    cross = lax.psum(dot_highest(panel_two.T, panel_one), ("row", "col"))
    weight_one = dot_highest(factor_one.T, panel_one.T)
    weight_two = dot_highest(factor_two.T, panel_two.T - dot_highest(cross, weight_one))
    weights = jnp.concatenate([weight_two, weight_one], axis=0)
    high, low = split_bf16(jnp.concatenate([panel_two, panel_one], axis=1))

    ordered, projected = orthogonalize(active, (owner ^ column_index)[:, None], factors, high, low, blocks)
    projected = sum_everywhere(projected.reshape(column_count * KD, -1))
    ordered = ordered.reshape(column_count * KD, width)
    result = ordered - jnp.dot(
        projected, weights, precision=lax.Precision.HIGH, preferred_element_type=jnp.float32
    )

    def row_block(k):
        return lax.dynamic_slice_in_dim(result, (column_index ^ k) * KD, KD, 0)

    gathered = jnp.zeros((KD, column_count * width), jnp.float32)
    for k in range(column_count):
        piece = swap(row_block(k), "col", k) if k else row_block(0)
        gathered = lax.dynamic_update_slice_in_dim(gathered, piece, (column_index ^ k) * width, 1)
    return gathered


def solution(mesh):
    placed = (
        P("col", "row"),
        P(),
        P("col", None),
        P(("row", "col"), None),
        P(),
        P(("row", "col"), None),
        P(),
    )
    return jax.shard_map(
        body, mesh=mesh, in_specs=placed, out_specs=P("col", "row"), check_vma=False
    )
```

```python
import functools
import math

import jax
import jax.numpy as jnp
from jax import lax
from jax.experimental import pallas as pl
from jax.experimental.pallas import tpu as pltpu
from jax.sharding import PartitionSpec as P

N = 81920
NB = 16
KD = 128
CMAX = 32
STEP = 64

highest = lax.Precision.HIGHEST


def dot_highest(a, b):
    return jnp.dot(a, b, precision=highest, preferred_element_type=jnp.float32)


def split_bf16(x):
    high = lax.reduce_precision(x, exponent_bits=8, mantissa_bits=7)
    return high.astype(jnp.bfloat16), (x - high).astype(jnp.bfloat16)


def swap(x, axis, step):
    size = lax.axis_size(axis)
    return lax.ppermute(x, axis, [(i, i ^ step) for i in range(size)])


def scatter_sum(x, axis, steps, index, unit):
    rows = x.shape[0] // (len(steps) + 1)
    total = lax.dynamic_slice_in_dim(x, index * rows, rows, 0)
    for step in steps:
        part = lax.dynamic_slice_in_dim(x, (index ^ step) * rows, rows, 0)
        total = total + swap(part, axis, step * unit)
    return total


def gather_rows(x, axis, steps, index, unit):
    rows = x.shape[0]
    whole = jnp.zeros(((len(steps) + 1) * rows,) + x.shape[1:], x.dtype)
    whole = lax.dynamic_update_slice_in_dim(whole, x, index * rows, 0)
    for step in steps:
        whole = lax.dynamic_update_slice_in_dim(whole, swap(x, axis, step * unit), (index ^ step) * rows, 0)
    return whole


def sum_everywhere(x):
    row_index, col_index = lax.axis_index("row"), lax.axis_index("col")
    stages = (
        ("row", range(1, 2), row_index % 2, 1),
        ("row", range(1, lax.axis_size("row") // 2), row_index // 2, 2),
        ("col", range(1, lax.axis_size("col")), col_index, 1),
    )
    for axis, steps, index, unit in stages:
        x = scatter_sum(x, axis, steps, index, unit)
    for axis, steps, index, unit in reversed(stages):
        x = gather_rows(x, axis, steps, index, unit)
    return x


def inverse_factor(gram_full, labels, is_alive):
    same_group = (labels[:, None] == labels[None, :]) & is_alive[:, None] & is_alive[None, :]
    alive_float = is_alive.astype(jnp.float32)
    masked = jnp.where(same_group, gram_full, 0.0) + jnp.diag(1.0 - alive_float)
    lower_factor = jnp.linalg.cholesky(masked)
    scaled_eye = math.sqrt(N) * jnp.eye(masked.shape[0], dtype=jnp.float32)
    return jax.scipy.linalg.solve_triangular(lower_factor, scaled_eye, lower=True)


def take_band(inverse):
    padded = jnp.pad(inverse, ((0, 0), (CMAX, 0)))
    groups = range(0, inverse.shape[0], CMAX)
    return jnp.concatenate([padded[g : g + CMAX, g : g + 2 * CMAX] for g in groups], axis=0)


def spread_band(bands, capacity):
    bands = bands.reshape(-1, capacity, 2 * CMAX)
    groups = [
        jnp.pad(bands[:, g : g + CMAX], ((0, 0), (0, 0), (g, capacity - CMAX - g)))
        for g in range(0, capacity, CMAX)
    ]
    return jnp.concatenate(groups, axis=1)[:, :, CMAX:].reshape(-1, capacity)


def orthogonal_kernel(count, split, base_ref, owner_ref, factor_ref, high_ref, low_ref, *refs):
    blocks, rest = refs[:count], refs[count:]
    ordered_ref, projected_ref, total = rest[-3:]
    rank_total, capacity = ordered_ref.shape[0], factor_ref.shape[1]
    total[...] = jnp.zeros_like(total)
    for k in range(count):
        block = blocks[k][...]
        if split:
            begin = k % 2 * split
            beyond = rest[k][...] if k < 2 else rest[2][k // 2 - 1, begin : begin + split, :]
            block = jnp.concatenate([block, beyond], axis=0)
        block_high = block.astype(jnp.bfloat16)
        block_low = (block - block_high.astype(jnp.float32)).astype(jnp.bfloat16)
        ranks = pl.ds(pl.multiple_of(base_ref[k], 8), capacity + 2 * 8)
        factor = jnp.where(owner_ref[ranks, :] == k, factor_ref[ranks, :], 0.0)
        factor_high = factor.astype(jnp.bfloat16)
        factor_low = (factor - factor_high.astype(jnp.float32)).astype(jnp.bfloat16)
        part = jnp.dot(factor_high, block_high, preferred_element_type=jnp.float32)
        part += jnp.dot(factor_high, block_low, preferred_element_type=jnp.float32)
        part += jnp.dot(factor_low, block_high, preferred_element_type=jnp.float32)
        total[ranks, :] += part

    value = total[:rank_total, :]
    ordered_ref[...] = value
    value_high = value.astype(jnp.bfloat16)
    value_low = (value - value_high.astype(jnp.float32)).astype(jnp.bfloat16)
    projected = jnp.dot(value_high, high_ref[...], preferred_element_type=jnp.float32)
    projected += jnp.dot(value_low, high_ref[...], preferred_element_type=jnp.float32)
    projected += jnp.dot(value_high, low_ref[...], preferred_element_type=jnp.float32)

    @pl.when(pl.program_id(0) == 0)
    def _():
        projected_ref[...] = projected

    @pl.when(pl.program_id(0) > 0)
    def _():
        projected_ref[...] += projected


def orthogonalize(rank_total, base, owner, factors, high, low, blocks, excess):
    count, (rows, width) = len(blocks), blocks[0].shape
    reflectors, (padded, capacity) = high.shape[1], factors.shape
    tile = max(t for t in (128, 256, 512) if width % t == 0)
    whole = lambda shape: pl.BlockSpec(shape, lambda n, *_: (0,) * len(shape))
    column = lambda shape: pl.BlockSpec(shape + (tile,), lambda n, *_: (0,) * len(shape) + (n,))
    return pl.pallas_call(
        functools.partial(orthogonal_kernel, count, rows if excess else 0),
        grid_spec=pltpu.PrefetchScalarGridSpec(
            num_scalar_prefetch=1,
            grid=(width // tile,),
            in_specs=[whole((padded, 1)), whole((padded, capacity))]
            + [pl.BlockSpec((tile, reflectors), lambda n, *_: (n, 0))] * 2
            + [column((rows,))] * count
            + [column(e.shape[:-1]) for e in excess],
            out_specs=[column((rank_total,)), whole((rank_total, reflectors))],
            scratch_shapes=[pltpu.VMEM((padded, tile), jnp.float32)],
        ),
        out_shape=[
            jax.ShapeDtypeStruct((rank_total, width), jnp.float32),
            jax.ShapeDtypeStruct((rank_total, reflectors), jnp.float32),
        ],
        compiler_params=pltpu.CompilerParams(vmem_limit_bytes=56 * 2**20),
    )(base, owner, factors, high, low, *blocks, *excess)


def correct_kernel(count, target_ref, ordered_ref, projected_ref, weight_ref, *refs):
    pieces, high, low, result = refs[:count], refs[-3], refs[-2], refs[-1]

    @pl.when(pl.program_id(0) == 0)
    def _():
        projected = projected_ref[...]
        rounded = projected.astype(jnp.bfloat16)
        high[...] = rounded
        low[...] = (projected - rounded.astype(jnp.float32)).astype(jnp.bfloat16)

    weight = weight_ref[...]
    weight_high = weight.astype(jnp.bfloat16)
    weight_low = (weight - weight_high.astype(jnp.float32)).astype(jnp.bfloat16)
    product = jnp.dot(high[...], weight_high, preferred_element_type=jnp.float32)
    product += jnp.dot(low[...], weight_high, preferred_element_type=jnp.float32)
    product += jnp.dot(high[...], weight_low, preferred_element_type=jnp.float32)
    result[...] = ordered_ref[...] - product
    for k in range(count):
        for j in range(KD // NB):
            rows = pl.ds(pl.multiple_of((j * count + target_ref[k]) * NB, NB), NB)
            pieces[k][j * NB : (j + 1) * NB, :] = result[rows, :]


def correct(target, ordered, projected, weights):
    count, (rank_total, width), reflectors = target.shape[0], ordered.shape, weights.shape[0]
    tile = max(t for t in (128, 256, 512) if width % t == 0)
    column = lambda rows: pl.BlockSpec((rows, tile), lambda n, *_: (0, n))
    return pl.pallas_call(
        functools.partial(correct_kernel, count),
        grid_spec=pltpu.PrefetchScalarGridSpec(
            num_scalar_prefetch=1,
            grid=(width // tile,),
            in_specs=[
                column(rank_total),
                pl.BlockSpec((rank_total, reflectors), lambda n, *_: (0, 0)),
                column(reflectors),
            ],
            out_specs=[column(KD)] * count,
            scratch_shapes=[pltpu.VMEM((rank_total, reflectors), jnp.bfloat16)] * 2
            + [pltpu.VMEM((rank_total, tile), jnp.float32)],
        ),
        out_shape=[jax.ShapeDtypeStruct((KD, width), jnp.float32)] * count,
        compiler_params=pltpu.CompilerParams(vmem_limit_bytes=56 * 2**20),
    )(target, ordered, projected, weights)


def pair_excess(raw_vectors, half, width, pairs):
    column_index = lax.axis_index("col")
    parity = column_index % 2

    def side(which):
        cut = [
            lax.dynamic_slice(raw_vectors, (half, (2 * p + which) * width), (half, width)) for p in range(pairs)
        ]
        return jnp.stack(cut)

    first = lax.dynamic_slice(raw_vectors, (0, (column_index ^ 1) * width), (half, width))
    return side(parity), swap(jnp.concatenate([side(1 - parity), first[None]]), "col", 1)


def send_excess(own, other, beyond, pairs):
    pair_index, parity = lax.axis_index("col") // 2, lax.axis_index("col") % 2
    half, width = own.shape[1:]
    steps = (beyond.reshape(pairs, 2) + STEP - 1) // STEP
    own_steps = jnp.where(parity == 0, steps[:, 0], steps[:, 1])
    total_steps = jnp.sum(steps, axis=1)
    order = jnp.arange(pairs, dtype=jnp.int32)
    held = jnp.zeros((pairs - 1, 2 * half + STEP, width), jnp.float32)

    def branch(bits):
        def send(chunks):
            got = []
            for k in range(1, pairs):
                links = [(s, s ^ (2 * k)) for s in range(2 * pairs) if bits >> (s // 2) & 1]
                got.append(lax.ppermute(chunks[k - 1], "col", links) if links else chunks[k - 1])
            return got

        return send

    def step(carry):
        i, held = carry
        going = i < total_steps
        place = jnp.where(i < own_steps, i, half // STEP + i - own_steps)
        place = jnp.where(going, place, 2 * half // STEP) * STEP
        begin = jnp.sum(jnp.where(order == pair_index, place, 0))

        def chunk(k):
            from_own = lax.dynamic_slice(own, (pair_index ^ k, begin, 0), (1, STEP, width))
            from_other = lax.dynamic_slice(other, (pair_index ^ k, begin - half, 0), (1, STEP, width))
            return jnp.where(begin < half, from_own, from_other)

        bits = jnp.sum(jnp.where(going, 1 << order, 0))
        got = lax.switch(bits, [branch(b) for b in range(1 << pairs)], [chunk(k) for k in range(1, pairs)])
        for k in range(1, pairs):
            at = jnp.sum(jnp.where(order == (pair_index ^ k), place, 0))
            held = lax.dynamic_update_slice(held, got[k - 1], (k - 1, at, 0))
        return i + 1, held

    return lax.while_loop(lambda carry: carry[0] < jnp.max(total_steps), step, (jnp.int32(0), held))[1]


def body(raw_vectors, interval_count, cluster_of, panel_one, factor_one, panel_two, factor_two):
    column_count = lax.axis_size("col")
    column_index = lax.axis_index("col")
    capacity = raw_vectors.shape[0]
    width = panel_one.shape[0]
    rank_total = column_count * KD
    columns = jnp.arange(column_count, dtype=jnp.int32)
    pairs = column_count // 2
    balanced = pairs < 1
    half = capacity // 2
    sent_rows = half if balanced else capacity

    def column_block(k):
        return lax.dynamic_slice(raw_vectors, (0, (column_index ^ k) * width), (sent_rows, width))

    blocks = {0: column_block(0)}
    if balanced:
        own, other = pair_excess(raw_vectors, half, width, pairs)
        blocks[1] = other[pairs]
    for k in sorted(set(range(1, column_count)) - set(blocks), key=lambda k: (-(k.bit_length()), k & 1, k)):
        blocks[k] = swap(column_block(k), "col", k)
    blocks = [blocks[k] for k in range(column_count)]

    own_count = jnp.sum(jnp.where(columns == column_index, interval_count, 0))
    is_alive = jnp.arange(capacity, dtype=jnp.int32) < own_count
    gram_rows, left_panel, blocks[1] = lax.optimization_barrier((raw_vectors, panel_two, blocks[1]))
    gram_full = lax.psum(dot_highest(gram_rows, gram_rows.T), "row")
    cross = lax.psum(dot_highest(left_panel.T, panel_one), ("row", "col"))
    inverse = inverse_factor(gram_full, cluster_of[0], is_alive)
    inverses = spread_band(lax.all_gather(take_band(inverse), "col", axis=0, tiled=True), capacity)

    padded = rank_total + capacity + 2 * 8
    ranks = jnp.arange(padded, dtype=jnp.int32)
    interval_end = jnp.cumsum(interval_count).astype(jnp.int32)
    interval_start = interval_end - interval_count
    owner = jnp.sum((interval_end[None, :] <= ranks[:, None]).astype(jnp.int32), axis=1)
    owner_start = jnp.sum(jnp.where(columns[None, :] == owner[:, None], interval_start[None, :], 0), axis=1)
    slot = jnp.where(owner < column_count, owner * capacity + ranks - owner_start, 0)
    factors = jnp.take(inverses, slot, axis=0)
    factors, cross = lax.optimization_barrier((factors, cross))
    owner = jnp.where(owner < column_count, owner ^ column_index, -1)[:, None]
    base = jnp.take(interval_start // 8 * 8, columns ^ column_index)

    weight_one = dot_highest(factor_one.T, panel_one.T)
    weight_two = dot_highest(factor_two.T, panel_two.T - dot_highest(cross, weight_one))
    weights = jnp.concatenate([weight_two, weight_one], axis=0)
    high, low = split_bf16(jnp.concatenate([panel_two, panel_one], axis=1))

    excess = []
    if balanced:
        own, other, factors, weights, blocks = lax.optimization_barrier((own, other, factors, weights, blocks))
        mine = [lax.dynamic_index_in_dim(x, column_index // 2, 0, keepdims=False) for x in (own, other)]
        excess = mine + [send_excess(own, other, jnp.maximum(interval_count - half, 0), pairs)]

    ordered, projected = orthogonalize(rank_total, base, owner, factors, high, low, blocks, excess)
    pieces = correct(columns ^ column_index, ordered, sum_everywhere(projected), weights)
    gathered = jnp.zeros((KD, column_count * width), jnp.float32)
    for k in sorted(range(column_count), key=lambda k: (-(k.bit_length()), k & 1, k)):
        piece = swap(pieces[k], "col", k) if k else pieces[0]
        gathered = lax.dynamic_update_slice_in_dim(gathered, piece, (column_index ^ k) * width, 1)
    return gathered


def solution(mesh):
    placed = (
        P("col", "row"),
        P(),
        P("col", None),
        P(("row", "col"), None),
        P(),
        P(("row", "col"), None),
        P(),
    )
    return jax.shard_map(
        body, mesh=mesh, in_specs=placed, out_specs=P("col", "row"), check_vma=False
    )
```

```python
import functools
import itertools
import math

import jax
import jax.numpy as jnp
from jax import lax
from jax.experimental import pallas as pl
from jax.experimental.pallas import tpu as pltpu
from jax.sharding import PartitionSpec as P

N = 81920
NB = 16
KD = 128
CMAX = 32

highest = lax.Precision.HIGHEST


def dot_highest(a, b):
    return jnp.dot(a, b, precision=highest, preferred_element_type=jnp.float32)


def split_bf16(x):
    high = lax.reduce_precision(x, exponent_bits=8, mantissa_bits=7)
    return high.astype(jnp.bfloat16), (x - high).astype(jnp.bfloat16)


def swap(x, axis, step):
    size = lax.axis_size(axis)
    return lax.ppermute(x, axis, [(i, i ^ step) for i in range(size)])


def scatter_sum(x, axis, steps, index, unit):
    rows = x.shape[0] // (len(steps) + 1)
    total = lax.dynamic_slice_in_dim(x, index * rows, rows, 0)
    for step in steps:
        part = lax.dynamic_slice_in_dim(x, (index ^ step) * rows, rows, 0)
        total = total + swap(part, axis, step * unit)
    return total


def gather_rows(x, axis, steps, index, unit):
    rows = x.shape[0]
    whole = jnp.zeros(((len(steps) + 1) * rows,) + x.shape[1:], x.dtype)
    whole = lax.dynamic_update_slice_in_dim(whole, x, index * rows, 0)
    for step in steps:
        whole = lax.dynamic_update_slice_in_dim(whole, swap(x, axis, step * unit), (index ^ step) * rows, 0)
    return whole


def sum_everywhere(x):
    row_index, col_index = lax.axis_index("row"), lax.axis_index("col")
    stages = (
        ("row", range(1, 2), row_index % 2, 1),
        ("row", range(1, lax.axis_size("row") // 2), row_index // 2, 2),
        ("col", range(1, lax.axis_size("col")), col_index, 1),
    )
    for axis, steps, index, unit in stages:
        x = scatter_sum(x, axis, steps, index, unit)
    for axis, steps, index, unit in reversed(stages):
        x = gather_rows(x, axis, steps, index, unit)
    return x


def inverse_factor(gram_full, labels, is_alive):
    same_group = (labels[:, None] == labels[None, :]) & is_alive[:, None] & is_alive[None, :]
    alive_float = is_alive.astype(jnp.float32)
    masked = jnp.where(same_group, gram_full, 0.0) + jnp.diag(1.0 - alive_float)
    lower_factor = jnp.linalg.cholesky(masked)
    scaled_eye = math.sqrt(N) * jnp.eye(masked.shape[0], dtype=jnp.float32)
    return jax.scipy.linalg.solve_triangular(lower_factor, scaled_eye, lower=True)


def take_band(inverse):
    padded = jnp.pad(inverse, ((0, 0), (CMAX, 0)))
    groups = range(0, inverse.shape[0], CMAX)
    return jnp.concatenate([padded[g : g + CMAX, g : g + 2 * CMAX] for g in groups], axis=0)


def spread_band(bands, capacity):
    bands = bands.reshape(-1, capacity, 2 * CMAX)
    groups = [
        jnp.pad(bands[:, g : g + CMAX], ((0, 0), (0, 0), (g, capacity - CMAX - g)))
        for g in range(0, capacity, CMAX)
    ]
    return jnp.concatenate(groups, axis=1)[:, :, CMAX:].reshape(-1, capacity)


def orthogonal_kernel(count, split, base_ref, second_ref, owner_ref, factor_ref, high_ref, low_ref, *refs):
    blocks, rest = refs[:count], refs[count:]
    ordered_ref, projected_ref, total = rest[-3:]
    rank_total, capacity = ordered_ref.shape[0], factor_ref.shape[1]
    total[...] = jnp.zeros_like(total)
    for k in range(count):
        block = blocks[k][...]
        if split:
            beyond = rest[k][...] if k < 2 else rest[k // 2 * 2][...]
            if k > 2 and k % 2:
                beyond = jnp.where(second_ref[k] > 0, rest[k][...], beyond)
            block = jnp.concatenate([block, beyond], axis=0)
        block_high = block.astype(jnp.bfloat16)
        block_low = (block - block_high.astype(jnp.float32)).astype(jnp.bfloat16)
        ranks = pl.ds(pl.multiple_of(base_ref[k], 8), capacity + 2 * 8)
        factor = jnp.where(owner_ref[ranks, :] == k, factor_ref[ranks, :], 0.0)
        factor_high = factor.astype(jnp.bfloat16)
        factor_low = (factor - factor_high.astype(jnp.float32)).astype(jnp.bfloat16)
        part = jnp.dot(factor_high, block_high, preferred_element_type=jnp.float32)
        part += jnp.dot(factor_high, block_low, preferred_element_type=jnp.float32)
        part += jnp.dot(factor_low, block_high, preferred_element_type=jnp.float32)
        total[ranks, :] += part

    value = total[:rank_total, :]
    ordered_ref[...] = value
    value_high = value.astype(jnp.bfloat16)
    value_low = (value - value_high.astype(jnp.float32)).astype(jnp.bfloat16)
    projected = jnp.dot(value_high, high_ref[...], preferred_element_type=jnp.float32)
    projected += jnp.dot(value_low, high_ref[...], preferred_element_type=jnp.float32)
    projected += jnp.dot(value_high, low_ref[...], preferred_element_type=jnp.float32)

    @pl.when(pl.program_id(0) == 0)
    def _():
        projected_ref[...] = projected

    @pl.when(pl.program_id(0) > 0)
    def _():
        projected_ref[...] += projected


def orthogonalize(rank_total, base, second, owner, factors, high, low, blocks, excess):
    count, (rows, width) = len(blocks), blocks[0].shape
    reflectors, (padded, capacity) = high.shape[1], factors.shape
    tile = max(t for t in (128, 256, 512) if width % t == 0)
    whole = lambda shape: pl.BlockSpec(shape, lambda n, *_: (0,) * len(shape))
    column = lambda shape: pl.BlockSpec(shape + (tile,), lambda n, *_: (0,) * len(shape) + (n,))
    return pl.pallas_call(
        functools.partial(orthogonal_kernel, count, rows if excess else 0),
        grid_spec=pltpu.PrefetchScalarGridSpec(
            num_scalar_prefetch=2,
            grid=(width // tile,),
            in_specs=[whole((padded, 1)), whole((padded, capacity))]
            + [pl.BlockSpec((tile, reflectors), lambda n, *_: (n, 0))] * 2
            + [column((rows,))] * count
            + [column(e.shape[:-1]) for e in excess],
            out_specs=[column((rank_total,)), whole((rank_total, reflectors))],
            scratch_shapes=[pltpu.VMEM((padded, tile), jnp.float32)],
        ),
        out_shape=[
            jax.ShapeDtypeStruct((rank_total, width), jnp.float32),
            jax.ShapeDtypeStruct((rank_total, reflectors), jnp.float32),
        ],
        compiler_params=pltpu.CompilerParams(vmem_limit_bytes=56 * 2**20),
    )(base, second, owner, factors, high, low, *blocks, *excess)


def correct_kernel(count, target_ref, ordered_ref, projected_ref, weight_ref, *refs):
    pieces, high, low, result = refs[:count], refs[-3], refs[-2], refs[-1]

    @pl.when(pl.program_id(0) == 0)
    def _():
        projected = projected_ref[...]
        rounded = projected.astype(jnp.bfloat16)
        high[...] = rounded
        low[...] = (projected - rounded.astype(jnp.float32)).astype(jnp.bfloat16)

    weight = weight_ref[...]
    weight_high = weight.astype(jnp.bfloat16)
    weight_low = (weight - weight_high.astype(jnp.float32)).astype(jnp.bfloat16)
    product = jnp.dot(high[...], weight_high, preferred_element_type=jnp.float32)
    product += jnp.dot(low[...], weight_high, preferred_element_type=jnp.float32)
    product += jnp.dot(high[...], weight_low, preferred_element_type=jnp.float32)
    result[...] = ordered_ref[...] - product
    for k in range(count):
        for j in range(KD // NB):
            rows = pl.ds(pl.multiple_of((j * count + target_ref[k]) * NB, NB), NB)
            pieces[k][j * NB : (j + 1) * NB, :] = result[rows, :]


def correct(target, ordered, projected, weights):
    count, (rank_total, width), reflectors = target.shape[0], ordered.shape, weights.shape[0]
    tile = max(t for t in (128, 256, 512) if width % t == 0)
    column = lambda rows: pl.BlockSpec((rows, tile), lambda n, *_: (0, n))
    return pl.pallas_call(
        functools.partial(correct_kernel, count),
        grid_spec=pltpu.PrefetchScalarGridSpec(
            num_scalar_prefetch=1,
            grid=(width // tile,),
            in_specs=[
                column(rank_total),
                pl.BlockSpec((rank_total, reflectors), lambda n, *_: (0, 0)),
                column(reflectors),
            ],
            out_specs=[column(KD)] * count,
            scratch_shapes=[pltpu.VMEM((rank_total, reflectors), jnp.bfloat16)] * 2
            + [pltpu.VMEM((rank_total, tile), jnp.float32)],
        ),
        out_shape=[jax.ShapeDtypeStruct((KD, width), jnp.float32)] * count,
        compiler_params=pltpu.CompilerParams(vmem_limit_bytes=56 * 2**20),
    )(target, ordered, projected, weights)


def pair_excess(raw_vectors, half, width, pairs):
    column_index = lax.axis_index("col")
    parity = column_index % 2

    def side(which):
        cut = [
            lax.dynamic_slice(raw_vectors, (half, (2 * p + which) * width), (half, width)) for p in range(pairs)
        ]
        return jnp.stack(cut)

    first = lax.dynamic_slice(raw_vectors, (0, (column_index ^ 1) * width), (half, width))
    return side(parity), swap(jnp.concatenate([side(1 - parity), first[None]]), "col", 1)


def link_load(plan):
    loads = []
    for cut in range(1, len(plan)):
        loads += [sum(plan[:cut]) * (len(plan) - cut), sum(plan[cut:]) * cut]
    return max(loads)


def excess_plans(pairs):
    tuples = list(itertools.product(range(3), repeat=pairs))
    chosen = []
    for need in tuples:
        covers = [p for p in tuples if all(a >= b for a, b in zip(p, need)) and link_load(p) == link_load(need)]
        chosen.append(max(covers, key=lambda p: (sum(p), p)))
    plans = sorted(set(chosen))
    return [plans.index(p) for p in chosen], plans


def send_excess(first, other, heavy, pairs):
    pair_index = lax.axis_index("col") // 2
    table, plans = excess_plans(pairs)
    used = jnp.sum(heavy.reshape(pairs, 2).astype(jnp.int32), axis=1)
    index = jnp.sum(used * jnp.array([3 ** (pairs - 1 - p) for p in range(pairs)], jnp.int32))

    def block(x, k):
        return lax.dynamic_index_in_dim(x, pair_index ^ k, 0, keepdims=False)

    def branch(plan):
        def send(first, other):
            got = []
            for k in range(1, pairs):
                for level, x in enumerate((first, other)):
                    links = [(s, s ^ (2 * k)) for s in range(2 * pairs) if plan[s // 2] > level]
                    got.append(lax.ppermute(block(x, k), "col", links) if links else block(x, k))
            return got

        return send

    got = lax.switch(jnp.take(jnp.array(table, jnp.int32), index), [branch(p) for p in plans], first, other)
    return got, used


def body(raw_vectors, interval_count, cluster_of, panel_one, factor_one, panel_two, factor_two):
    column_count = lax.axis_size("col")
    column_index = lax.axis_index("col")
    capacity = raw_vectors.shape[0]
    width = panel_one.shape[0]
    rank_total = column_count * KD
    columns = jnp.arange(column_count, dtype=jnp.int32)
    pairs = column_count // 2
    balanced = pairs <= 4
    half = capacity // 2
    sent_rows = half if balanced else capacity

    def column_block(k):
        return lax.dynamic_slice(raw_vectors, (0, (column_index ^ k) * width), (sent_rows, width))

    blocks = {0: column_block(0)}
    if balanced:
        own, other = pair_excess(raw_vectors, half, width, pairs)
        blocks[1] = other[pairs]
        for k in (2, 3):
            blocks[k] = swap(column_block(k), "col", k)
    for k in sorted(set(range(1, column_count)) - set(blocks), key=lambda k: (-(k.bit_length()), k & 1, k)):
        blocks[k] = swap(column_block(k), "col", k)
    blocks = [blocks[k] for k in range(column_count)]

    own_count = jnp.sum(jnp.where(columns == column_index, interval_count, 0))
    is_alive = jnp.arange(capacity, dtype=jnp.int32) < own_count
    tied = (2, 3) if balanced else (1,)
    first_blocks = [blocks[k] for k in tied]
    gram_rows, left_panel, first_blocks = lax.optimization_barrier((raw_vectors, panel_two, first_blocks))
    for k, block in zip(tied, first_blocks):
        blocks[k] = block
    gram_full = lax.psum(dot_highest(gram_rows, gram_rows.T), "row")
    cross = lax.psum(dot_highest(left_panel.T, panel_one), ("row", "col"))
    inverse = inverse_factor(gram_full, cluster_of[0], is_alive)
    inverses = spread_band(lax.all_gather(take_band(inverse), "col", axis=0, tiled=True), capacity)

    padded = rank_total + capacity + 2 * 8
    ranks = jnp.arange(padded, dtype=jnp.int32)
    interval_end = jnp.cumsum(interval_count).astype(jnp.int32)
    interval_start = interval_end - interval_count
    owner = jnp.sum((interval_end[None, :] <= ranks[:, None]).astype(jnp.int32), axis=1)
    owner_start = jnp.sum(jnp.where(columns[None, :] == owner[:, None], interval_start[None, :], 0), axis=1)
    slot = jnp.where(owner < column_count, owner * capacity + ranks - owner_start, 0)
    factors = jnp.take(inverses, slot, axis=0)
    owner = jnp.where(owner < column_count, owner ^ column_index, -1)[:, None]
    base = jnp.take(interval_start // 8 * 8, columns ^ column_index)

    high, low = split_bf16(jnp.concatenate([panel_two, panel_one], axis=1))

    excess, second = [], jnp.zeros((column_count,), jnp.int32)
    if balanced:
        heavy = interval_count > half
        excess = [lax.dynamic_index_in_dim(x, column_index // 2, 0, keepdims=False) for x in (own, other)]
        first = jnp.where(jnp.any(heavy & (columns == column_index)), own, other[:pairs])
        first, other, factors, blocks, excess = lax.optimization_barrier((first, other, factors, blocks, excess))
        got, used = send_excess(first, other, heavy, pairs)
        got, cross = lax.optimization_barrier((got, cross))
        excess += got
        second = (jnp.take(used, (columns ^ column_index) // 2) == 2).astype(jnp.int32)

    weight_one = dot_highest(factor_one.T, panel_one.T)
    weight_two = dot_highest(factor_two.T, panel_two.T - dot_highest(cross, weight_one))
    weights = jnp.concatenate([weight_two, weight_one], axis=0)
    ordered, projected = orthogonalize(rank_total, base, second, owner, factors, high, low, blocks, excess)
    pieces = correct(columns ^ column_index, ordered, sum_everywhere(projected), weights)
    gathered = jnp.zeros((KD, column_count * width), jnp.float32)
    for k in sorted(range(column_count), key=lambda k: (-(k.bit_length()), k & 1, k)):
        piece = swap(pieces[k], "col", k) if k else pieces[0]
        gathered = lax.dynamic_update_slice_in_dim(gathered, piece, (column_index ^ k) * width, 1)
    return gathered


def solution(mesh):
    placed = (
        P("col", "row"),
        P(),
        P("col", None),
        P(("row", "col"), None),
        P(),
        P(("row", "col"), None),
        P(),
    )
    return jax.shard_map(
        body, mesh=mesh, in_specs=placed, out_specs=P("col", "row"), check_vma=False
    )
```

```python
import functools
import itertools
import math

import jax
import jax.numpy as jnp
from jax import lax
from jax.experimental import pallas as pl
from jax.experimental.pallas import tpu as pltpu
from jax.sharding import PartitionSpec as P

N = 81920
NB = 16
KD = 128
CMAX = 32
LEVEL = 64
PLANS = (
    (1, 2, 1, 2), (2, 1, 2, 1), (2, 2, 2, 2), (1, 3, 3, 1), (2, 3, 2, 3), (3, 2, 3, 2), (1, 4, 4, 1), (4, 2, 2, 4),
    (4, 4, 4, 4),
)

highest = lax.Precision.HIGHEST


def dot_highest(a, b):
    return jnp.dot(a, b, precision=highest, preferred_element_type=jnp.float32)


def split_bf16(x):
    high = lax.reduce_precision(x, exponent_bits=8, mantissa_bits=7)
    return high.astype(jnp.bfloat16), (x - high).astype(jnp.bfloat16)


def swap(x, axis, step):
    size = lax.axis_size(axis)
    return lax.ppermute(x, axis, [(i, i ^ step) for i in range(size)])


def scatter_sum(x, axis, steps, index, unit):
    rows = x.shape[0] // (len(steps) + 1)
    total = lax.dynamic_slice_in_dim(x, index * rows, rows, 0)
    for step in steps:
        part = lax.dynamic_slice_in_dim(x, (index ^ step) * rows, rows, 0)
        total = total + swap(part, axis, step * unit)
    return total


def gather_rows(x, axis, steps, index, unit):
    rows = x.shape[0]
    whole = jnp.zeros(((len(steps) + 1) * rows,) + x.shape[1:], x.dtype)
    whole = lax.dynamic_update_slice_in_dim(whole, x, index * rows, 0)
    for step in steps:
        whole = lax.dynamic_update_slice_in_dim(whole, swap(x, axis, step * unit), (index ^ step) * rows, 0)
    return whole


def sum_everywhere(x):
    row_index, col_index = lax.axis_index("row"), lax.axis_index("col")
    stages = (
        ("row", range(1, 2), row_index % 2, 1),
        ("row", range(1, lax.axis_size("row") // 2), row_index // 2, 2),
        ("col", range(1, lax.axis_size("col")), col_index, 1),
    )
    for axis, steps, index, unit in stages:
        x = scatter_sum(x, axis, steps, index, unit)
    for axis, steps, index, unit in reversed(stages):
        x = gather_rows(x, axis, steps, index, unit)
    return x


def inverse_factor(gram_full, labels, is_alive):
    same_group = (labels[:, None] == labels[None, :]) & is_alive[:, None] & is_alive[None, :]
    alive_float = is_alive.astype(jnp.float32)
    masked = jnp.where(same_group, gram_full, 0.0) + jnp.diag(1.0 - alive_float)
    lower_factor = jnp.linalg.cholesky(masked)
    scaled_eye = math.sqrt(N) * jnp.eye(masked.shape[0], dtype=jnp.float32)
    return jax.scipy.linalg.solve_triangular(lower_factor, scaled_eye, lower=True)


def take_band(inverse):
    padded = jnp.pad(inverse, ((0, 0), (CMAX, 0)))
    groups = range(0, inverse.shape[0], CMAX)
    return jnp.concatenate([padded[g : g + CMAX, g : g + 2 * CMAX] for g in groups], axis=0)


def spread_band(bands, capacity):
    bands = bands.reshape(-1, capacity, 2 * CMAX)
    groups = [
        jnp.pad(bands[:, g : g + CMAX], ((0, 0), (0, 0), (g, capacity - CMAX - g)))
        for g in range(0, capacity, CMAX)
    ]
    return jnp.concatenate(groups, axis=1)[:, :, CMAX:].reshape(-1, capacity)


def orthogonal_kernel(count, split, base_ref, skip_ref, owner_ref, factor_ref, high_ref, low_ref, *refs):
    blocks, rest = refs[:count], refs[count:]
    ordered_ref, projected_ref, total = rest[-3:]
    rank_total, capacity = ordered_ref.shape[0], factor_ref.shape[1]
    total[...] = jnp.zeros_like(total)
    for k in range(count):
        block = blocks[k][...]
        if split:
            if k < 2:
                beyond = [rest[k][...]]
            else:
                per = (capacity - split) // LEVEL
                listed = [r[...] for r in rest[2 + (k // 2 - 1) * 2 * per : 2 + k // 2 * 2 * per]]
                beyond = listed[:per]
                for n in range(1, per + 1 if k % 2 else 1):
                    skipped = skip_ref[k] == n
                    beyond = [jnp.where(skipped, listed[i + n], b) for i, b in enumerate(beyond)]
            block = jnp.concatenate([block] + beyond, axis=0)
        block_high = block.astype(jnp.bfloat16)
        block_low = (block - block_high.astype(jnp.float32)).astype(jnp.bfloat16)
        ranks = pl.ds(pl.multiple_of(base_ref[k], 8), capacity + 2 * 8)
        factor = jnp.where(owner_ref[ranks, :] == k, factor_ref[ranks, :], 0.0)
        factor_high = factor.astype(jnp.bfloat16)
        factor_low = (factor - factor_high.astype(jnp.float32)).astype(jnp.bfloat16)
        part = jnp.dot(factor_high, block_high, preferred_element_type=jnp.float32)
        part += jnp.dot(factor_high, block_low, preferred_element_type=jnp.float32)
        part += jnp.dot(factor_low, block_high, preferred_element_type=jnp.float32)
        total[ranks, :] += part

    value = total[:rank_total, :]
    ordered_ref[...] = value
    value_high = value.astype(jnp.bfloat16)
    value_low = (value - value_high.astype(jnp.float32)).astype(jnp.bfloat16)
    projected = jnp.dot(value_high, high_ref[...], preferred_element_type=jnp.float32)
    projected += jnp.dot(value_low, high_ref[...], preferred_element_type=jnp.float32)
    projected += jnp.dot(value_high, low_ref[...], preferred_element_type=jnp.float32)

    @pl.when(pl.program_id(0) == 0)
    def _():
        projected_ref[...] = projected

    @pl.when(pl.program_id(0) > 0)
    def _():
        projected_ref[...] += projected


def orthogonalize(rank_total, base, skip, owner, factors, high, low, blocks, excess):
    count, (rows, width) = len(blocks), blocks[0].shape
    reflectors, (padded, capacity) = high.shape[1], factors.shape
    tile = max(t for t in (128, 256, 512) if width % t == 0)
    whole = lambda shape: pl.BlockSpec(shape, lambda n, *_: (0,) * len(shape))
    column = lambda shape: pl.BlockSpec(shape + (tile,), lambda n, *_: (0,) * len(shape) + (n,))
    return pl.pallas_call(
        functools.partial(orthogonal_kernel, count, rows if excess else 0),
        grid_spec=pltpu.PrefetchScalarGridSpec(
            num_scalar_prefetch=2,
            grid=(width // tile,),
            in_specs=[whole((padded, 1)), whole((padded, capacity))]
            + [pl.BlockSpec((tile, reflectors), lambda n, *_: (n, 0))] * 2
            + [column((rows,))] * count
            + [column(e.shape[:-1]) for e in excess],
            out_specs=[column((rank_total,)), whole((rank_total, reflectors))],
            scratch_shapes=[pltpu.VMEM((padded, tile), jnp.float32)],
        ),
        out_shape=[
            jax.ShapeDtypeStruct((rank_total, width), jnp.float32),
            jax.ShapeDtypeStruct((rank_total, reflectors), jnp.float32),
        ],
        compiler_params=pltpu.CompilerParams(vmem_limit_bytes=56 * 2**20),
    )(base, skip, owner, factors, high, low, *blocks, *excess)


def correct_kernel(count, target_ref, ordered_ref, projected_ref, weight_ref, *refs):
    pieces, high, low, result = refs[:count], refs[-3], refs[-2], refs[-1]

    @pl.when(pl.program_id(0) == 0)
    def _():
        projected = projected_ref[...]
        rounded = projected.astype(jnp.bfloat16)
        high[...] = rounded
        low[...] = (projected - rounded.astype(jnp.float32)).astype(jnp.bfloat16)

    weight = weight_ref[...]
    weight_high = weight.astype(jnp.bfloat16)
    weight_low = (weight - weight_high.astype(jnp.float32)).astype(jnp.bfloat16)
    product = jnp.dot(high[...], weight_high, preferred_element_type=jnp.float32)
    product += jnp.dot(low[...], weight_high, preferred_element_type=jnp.float32)
    product += jnp.dot(high[...], weight_low, preferred_element_type=jnp.float32)
    result[...] = ordered_ref[...] - product
    for k in range(count):
        for j in range(KD // NB):
            rows = pl.ds(pl.multiple_of((j * count + target_ref[k]) * NB, NB), NB)
            pieces[k][j * NB : (j + 1) * NB, :] = result[rows, :]


def correct(target, ordered, projected, weights):
    count, (rank_total, width), reflectors = target.shape[0], ordered.shape, weights.shape[0]
    tile = max(t for t in (128, 256, 512) if width % t == 0)
    column = lambda rows: pl.BlockSpec((rows, tile), lambda n, *_: (0, n))
    return pl.pallas_call(
        functools.partial(correct_kernel, count),
        grid_spec=pltpu.PrefetchScalarGridSpec(
            num_scalar_prefetch=1,
            grid=(width // tile,),
            in_specs=[
                column(rank_total),
                pl.BlockSpec((rank_total, reflectors), lambda n, *_: (0, 0)),
                column(reflectors),
            ],
            out_specs=[column(KD)] * count,
            scratch_shapes=[pltpu.VMEM((rank_total, reflectors), jnp.bfloat16)] * 2
            + [pltpu.VMEM((rank_total, tile), jnp.float32)],
        ),
        out_shape=[jax.ShapeDtypeStruct((KD, width), jnp.float32)] * count,
        compiler_params=pltpu.CompilerParams(vmem_limit_bytes=56 * 2**20),
    )(target, ordered, projected, weights)


def pair_excess(raw_vectors, half, width, pairs):
    column_index = lax.axis_index("col")
    parity = column_index % 2

    def side(which):
        cut = [
            lax.dynamic_slice(raw_vectors, (half, (2 * p + which) * width), (half, width)) for p in range(pairs)
        ]
        return jnp.stack(cut)

    first = lax.dynamic_slice(raw_vectors, (0, (column_index ^ 1) * width), (half, width))
    return side(parity), swap(jnp.concatenate([side(1 - parity), first[None]]), "col", 1)


def link_load(plan):
    loads = []
    for cut in range(1, len(plan)):
        loads += [sum(plan[:cut]) * (len(plan) - cut), sum(plan[cut:]) * cut]
    return max(loads)


def plan_table(levels):
    table = []
    for need in itertools.product(range(levels + 1), repeat=len(PLANS[0])):
        covers = [i for i, p in enumerate(PLANS) if all(a >= b for a, b in zip(p, need))]
        table.append(min(covers, key=lambda i: link_load(PLANS[i])))
    return table


def list_levels(own, other, own_blocks):
    pairs, half, width = own.shape
    per = half // LEVEL
    levels = []
    for level in range(2 * per):
        value = other[:pairs, (level % per) * LEVEL : (level % per + 1) * LEVEL]
        for n in range(per + 1):
            if n > level:
                choice = own[:, level * LEVEL : (level + 1) * LEVEL]
            elif level - n < per:
                choice = other[:pairs, (level - n) * LEVEL : (level - n + 1) * LEVEL]
            else:
                continue
            value = jnp.where(own_blocks == n, choice, value)
        levels.append(value)
    return levels


def send_excess(levels, used, pairs):
    pair_index = lax.axis_index("col") // 2
    count = len(levels)
    weights = jnp.array([(count + 1) ** (pairs - 1 - p) for p in range(pairs)], jnp.int32)
    plan = jnp.take(jnp.array(plan_table(count), jnp.int32), jnp.sum(used * weights))

    def block(x, k):
        return lax.dynamic_index_in_dim(x, pair_index ^ k, 0, keepdims=False)

    def branch(plan):
        def send(levels):
            got = []
            for k in range(1, pairs):
                for level, x in enumerate(levels):
                    links = [(s, s ^ (2 * k)) for s in range(2 * pairs) if plan[s // 2] > level]
                    got.append(lax.ppermute(block(x, k), "col", links) if links else block(x, k))
            return got

        return send

    return lax.switch(plan, [branch(p) for p in PLANS], levels)


def body(raw_vectors, interval_count, cluster_of, panel_one, factor_one, panel_two, factor_two):
    column_count = lax.axis_size("col")
    column_index = lax.axis_index("col")
    capacity = raw_vectors.shape[0]
    width = panel_one.shape[0]
    rank_total = column_count * KD
    columns = jnp.arange(column_count, dtype=jnp.int32)
    pairs = column_count // 2
    balanced = pairs == len(PLANS[0])
    half = capacity // 2
    sent_rows = half if balanced else capacity

    def column_block(k):
        return lax.dynamic_slice(raw_vectors, (0, (column_index ^ k) * width), (sent_rows, width))

    blocks = {0: column_block(0)}
    if balanced:
        own, other = pair_excess(raw_vectors, half, width, pairs)
        blocks[1] = other[pairs]
        for k in (2, 3):
            blocks[k] = swap(column_block(k), "col", k)
    for k in sorted(set(range(1, column_count)) - set(blocks), key=lambda k: (-(k.bit_length()), k & 1, k)):
        blocks[k] = swap(column_block(k), "col", k)
    blocks = [blocks[k] for k in range(column_count)]

    own_count = jnp.sum(jnp.where(columns == column_index, interval_count, 0))
    is_alive = jnp.arange(capacity, dtype=jnp.int32) < own_count
    tied = (2, 3) if balanced else (1,)
    first_blocks = [blocks[k] for k in tied]
    gram_rows, left_panel, first_blocks = lax.optimization_barrier((raw_vectors, panel_two, first_blocks))
    for k, block in zip(tied, first_blocks):
        blocks[k] = block
    gram_full = lax.psum(dot_highest(gram_rows, gram_rows.T), "row")
    cross = lax.psum(dot_highest(left_panel.T, panel_one), ("row", "col"))
    inverse = inverse_factor(gram_full, cluster_of[0], is_alive)
    inverses = spread_band(lax.all_gather(take_band(inverse), "col", axis=0, tiled=True), capacity)

    padded = rank_total + capacity + 2 * 8
    ranks = jnp.arange(padded, dtype=jnp.int32)
    interval_end = jnp.cumsum(interval_count).astype(jnp.int32)
    interval_start = interval_end - interval_count
    owner = jnp.sum((interval_end[None, :] <= ranks[:, None]).astype(jnp.int32), axis=1)
    owner_start = jnp.sum(jnp.where(columns[None, :] == owner[:, None], interval_start[None, :], 0), axis=1)
    slot = jnp.where(owner < column_count, owner * capacity + ranks - owner_start, 0)
    factors = jnp.take(inverses, slot, axis=0)
    owner = jnp.where(owner < column_count, owner ^ column_index, -1)[:, None]
    base = jnp.take(interval_start // 8 * 8, columns ^ column_index)

    high, low = split_bf16(jnp.concatenate([panel_two, panel_one], axis=1))

    excess, skip = [], jnp.zeros((column_count,), jnp.int32)
    if balanced:
        in_use = (jnp.maximum(interval_count - half, 0) + LEVEL - 1) // LEVEL
        own_blocks = jnp.sum(jnp.where(columns == column_index, in_use, 0))
        skip = jnp.take(in_use, columns ^ column_index ^ 1)
        excess = [lax.dynamic_index_in_dim(x, column_index // 2, 0, keepdims=False) for x in (own, other)]
        levels = list_levels(own, other, own_blocks)
        levels, factors, blocks, excess = lax.optimization_barrier((levels, factors, blocks, excess))
        got = send_excess(levels, jnp.sum(in_use.reshape(pairs, 2), axis=1), pairs)
        got, cross = lax.optimization_barrier((got, cross))
        excess += got

    weight_one = dot_highest(factor_one.T, panel_one.T)
    weight_two = dot_highest(factor_two.T, panel_two.T - dot_highest(cross, weight_one))
    weights = jnp.concatenate([weight_two, weight_one], axis=0)
    ordered, projected = orthogonalize(rank_total, base, skip, owner, factors, high, low, blocks, excess)
    pieces = correct(columns ^ column_index, ordered, sum_everywhere(projected), weights)
    gathered = jnp.zeros((KD, column_count * width), jnp.float32)
    for k in sorted(range(column_count), key=lambda k: (-(k.bit_length()), k & 1, k)):
        piece = swap(pieces[k], "col", k) if k else pieces[0]
        gathered = lax.dynamic_update_slice_in_dim(gathered, piece, (column_index ^ k) * width, 1)
    return gathered


def solution(mesh):
    placed = (
        P("col", "row"),
        P(),
        P("col", None),
        P(("row", "col"), None),
        P(),
        P(("row", "col"), None),
        P(),
    )
    return jax.shard_map(
        body, mesh=mesh, in_specs=placed, out_specs=P("col", "row"), check_vma=False
    )
```
